32 devices in a mesh: grp: 2 (over x), feat: 16 (over z, y, core).
Axes of the slice: x: 2, y: 2, z: 4, core: 2. Of those that a mesh axis runs over, the one named last changes fastest.
Arguments:
- inputs: bfloat16 [5120, 4096], P('feat', 'grp'), parts along dimension 1, may hold values from -6 to 6
- pattern: int32 [4, 16], P(None, 'feat'), may hold values 0 or 1
- rank_mask: int32 [128], replicated, may hold values 0 or 1
- up_diag: bfloat16 [20480, 320], P('feat'), may hold values from -0.15625 to 0.15625
- up_cross: bfloat16 [4, 20480, 320], P(None, 'feat'), may hold values from -0.15625 to 0.15625
- up_left: bfloat16 [20480, 128], P('feat'), may hold values from -0.5 to 0.5
- up_right: bfloat16 [5120, 128], P('feat'), may hold values from -0.078125 to 0.078125
- down_diag: bfloat16 [5120, 1280], P('feat'), may hold values from -0.078125 to 0.078125
- down_cross: bfloat16 [4, 5120, 1280], P(None, 'feat'), may hold values from -0.078125 to 0.078125
- down_left: bfloat16 [5120, 128], P('feat'), may hold values from -0.5 to 0.5
- down_right: bfloat16 [20480, 128], P('feat'), may hold values from -0.0390625 to 0.0390625
- cotangent: bfloat16 [5120, 4096], P('feat', 'grp'), parts along dimension 1, may hold values from -6 to 6
Outputs:
- output: bfloat16 [5120, 4096], P('feat', 'grp'), parts along dimension 1
- input_grad: bfloat16 [5120, 4096], P('feat', 'grp'), parts along dimension 1
- grad_up_diag: float32 [20480, 640], P('feat', 'grp'), parts along dimension 1
- grad_up_cross: float32 [4, 20480, 640], P(None, 'feat', 'grp'), parts along dimension 2
- grad_up_left: float32 [20480, 256], P('feat', 'grp'), parts along dimension 1
- grad_up_right: float32 [5120, 256], P('feat', 'grp'), parts along dimension 1
- grad_down_diag: float32 [5120, 2560], P('feat', 'grp'), parts along dimension 1
- grad_down_cross: float32 [4, 5120, 2560], P(None, 'feat', 'grp'), parts along dimension 2
- grad_down_left: float32 [5120, 256], P('feat', 'grp'), parts along dimension 1
- grad_down_right: float32 [20480, 256], P('feat', 'grp'), parts along dimension 1
The draws below stay inside these ranges and needn't reach their ends.
There are 2 independent parts, one for each index of `grp`. The reference program is written for one: setup_inputs(seed, part) draws one part's arguments, and reference() takes and returns one part's arrays. A program takes and returns all parts, laid end to end along the dimension named above; an argument that names none is the same for every part. Nothing has to cross between parts.
All inputs are finite; a program needn't handle non-finite values. No bound on the sum of `pattern` on one device may be relied on, other than what follows from the above.
Results may differ from the reference program's by a relative error of at most 0.0062.
Values may be sent and summed in bfloat16 or wider, within the bound.
A program may use at most 320 MiB of HBM per device.

```python
import jax
import jax.numpy as jnp
import numpy as np

D = 5120
FF = 20480
RANK = 128
LEVELS = 4
TOK = 2048
FEAT_DEV = 320
HID_DEV = 1280
N_FEAT = 16


def with_ends(drawn, rng, least, high):
    dims = drawn.shape
    spot = [jax.random.randint(jax.random.fold_in(rng, axis), (), 0, dims[axis]) for axis in range(len(dims))]
    drawn = drawn.at[tuple(spot)].set(least)
    longest = dims.index(max(dims))
    spot[longest] = (spot[longest] + 1) % dims[longest]
    return drawn.at[tuple(spot)].set(high)


def levels(rng, extent, cuts, least, top_value):
    def one(axis_at, shards_of):
        draws = jax.random.uniform(jax.random.fold_in(jax.random.fold_in(rng, 6), axis_at), (shards_of,), jnp.float32, least / len(cuts), top_value / len(cuts))
        return jnp.repeat(jnp.exp(draws), extent[axis_at] // shards_of).reshape((-1,) + (1,) * (len(extent) - axis_at - 1))

    gain = one(*cuts[0])
    for cut in cuts[1:]:
        gain = gain * one(*cut)
    return gain


def noise(key, shape, scale, reach, pieces=(), kind=jnp.bfloat16):
    values = jax.random.normal(key, shape, jnp.float32) * scale
    if len(pieces) > 0:
        values = levels(key, shape, pieces, -0.22, 0.18) * values
    return jnp.clip(values, min=-reach, max=reach).astype(kind)


def setup_inputs(seed: int = 0, part: int = 0) -> dict:
    splits = jax.random.split(jax.random.key(seed), 13)
    part_splits = jax.random.split(jax.random.fold_in(splits[12], part), 13)
    return {
        "inputs": noise(part_splits[0], (D, TOK), 1.0, 6.0, ((0, 16),)),
        "pattern": with_ends((jax.random.randint(splits[1], (LEVELS, N_FEAT), 0, 4) < 3).astype(jnp.int32), jax.random.fold_in(splits[1], 1), 0, 1),
        "rank_mask": with_ends((jax.random.randint(splits[2], (RANK,), 0, 4) < 3).astype(jnp.int32), jax.random.fold_in(splits[2], 1), 0, 1),
        "up_diag": noise(splits[3], (FF, FEAT_DEV), (FEAT_DEV * (LEVELS + 1)) ** -0.5, 0.15625, ((0, 16),)),
        "up_cross": noise(splits[4], (LEVELS, FF, FEAT_DEV), (FEAT_DEV * (LEVELS + 1)) ** -0.5, 0.15625, ((1, 16),)),
        "up_left": noise(splits[5], (FF, RANK), RANK ** -0.5, 0.5, ((0, 16),)),
        "up_right": noise(splits[6], (D, RANK), D ** -0.5, 0.078125, ((0, 16),)),
        "down_diag": noise(splits[7], (D, HID_DEV), (HID_DEV * (LEVELS + 1)) ** -0.5, 0.078125, ((0, 16),)),
        "down_cross": noise(splits[8], (LEVELS, D, HID_DEV), (HID_DEV * (LEVELS + 1)) ** -0.5, 0.078125, ((1, 16),)),
        "down_left": noise(splits[9], (D, RANK), RANK ** -0.5, 0.5, ((0, 16),)),
        "down_right": noise(splits[10], (FF, RANK), FF ** -0.5, 0.0390625, ((0, 16),)),
        "cotangent": noise(part_splits[11], (D, TOK), 1.0, 6.0, ((0, 16),)),
    }


def activate(values):
    return jax.nn.gelu(values, approximate=True)

def partners(level):
    shift = N_FEAT.bit_length() - 1 - LEVELS + level
    return np.arange(N_FEAT) ^ 1 << shift

def block_mul(weights, values):
    return jnp.einsum('nab,nbt->nat', weights.astype(jnp.float32), values.astype(jnp.float32))

def block_tmul(weights, values):
    return jnp.einsum('nba,nbt->nat', weights.astype(jnp.float32), values.astype(jnp.float32))

def block_outer(left, right):
    return jnp.einsum('nat,nbt->nab', left.astype(jnp.float32), right.astype(jnp.float32))

def reference(inputs, pattern, rank_mask, up_diag, up_cross, up_left, up_right, down_diag, down_cross, down_left, down_right, cotangent):
    count = N_FEAT
    rows = D // count
    hid = FF // count
    width = inputs.shape[1]
    in_blocks = inputs.reshape(count, rows, width)
    gates = pattern.astype(jnp.float32)
    keep = rank_mask.astype(jnp.float32)[:, None]
    up_d = up_diag.reshape(count, hid, rows)
    up_c = up_cross.reshape(LEVELS, count, hid, rows)
    down_d = down_diag.reshape(count, rows, hid)
    down_c = down_cross.reshape(LEVELS, count, rows, hid)
    pre_act = block_mul(up_d, in_blocks)
    for level in range(LEVELS):
        index = partners(level)
        pre_act = pre_act + gates[level][:, None, None] * block_mul(up_c[level], in_blocks[index])
    up_code = (jnp.dot(up_right.T, inputs, preferred_element_type=jnp.float32) * keep).astype(jnp.bfloat16)
    pre_act = pre_act + jnp.dot(up_left, up_code, preferred_element_type=jnp.float32).reshape(count, hid, width)
    hidden = activate(pre_act).astype(jnp.bfloat16)
    hidden_flat = hidden.reshape(FF, width)
    result = block_mul(down_d, hidden)
    for level in range(LEVELS):
        index = partners(level)
        result = result + gates[level][:, None, None] * block_mul(down_c[level], hidden[index])
    down_code = (jnp.dot(down_right.T, hidden_flat, preferred_element_type=jnp.float32) * keep).astype(jnp.bfloat16)
    result = result + jnp.dot(down_left, down_code, preferred_element_type=jnp.float32).reshape(count, rows, width)
    output = result.reshape(D, width).astype(jnp.bfloat16)
    cot_blocks = cotangent.reshape(count, rows, width)
    down_back = (jnp.dot(down_left.T, cotangent, preferred_element_type=jnp.float32) * keep).astype(jnp.bfloat16)
    hidden_grad = block_tmul(down_d, cot_blocks) + jnp.dot(down_right, down_back, preferred_element_type=jnp.float32).reshape(count, hid, width)
    for level in range(LEVELS):
        index = partners(level)
        scaled = gates[level][index][:, None, None] * down_c[level][index].astype(jnp.float32)
        hidden_grad = hidden_grad + block_tmul(scaled, cot_blocks[index])
    pre_grad = jax.vjp(activate, pre_act)[1](hidden_grad)[0].astype(jnp.bfloat16)
    pre_flat = pre_grad.reshape(FF, width)
    up_back = (jnp.dot(up_left.T, pre_flat, preferred_element_type=jnp.float32) * keep).astype(jnp.bfloat16)
    in_grad = block_tmul(up_d, pre_grad) + jnp.dot(up_right, up_back, preferred_element_type=jnp.float32).reshape(count, rows, width)
    for level in range(LEVELS):
        index = partners(level)
        scaled = gates[level][index][:, None, None] * up_c[level][index].astype(jnp.float32)
        in_grad = in_grad + block_tmul(scaled, pre_grad[index])
    input_grad = in_grad.reshape(D, width).astype(jnp.bfloat16)
    grad_up_diag = block_outer(pre_grad, in_blocks).reshape(FF, rows)
    grad_up_cross = jnp.stack([gates[level][:, None, None] * block_outer(pre_grad, in_blocks[partners(level)]) for level in range(LEVELS)]).reshape(LEVELS, FF, rows)
    grad_up_left = jnp.dot(pre_flat, up_code.T, preferred_element_type=jnp.float32)
    grad_up_right = jnp.dot(inputs, up_back.T, preferred_element_type=jnp.float32)
    grad_down_diag = block_outer(cot_blocks, hidden).reshape(D, hid)
    grad_down_cross = jnp.stack([gates[level][:, None, None] * block_outer(cot_blocks, hidden[partners(level)]) for level in range(LEVELS)]).reshape(LEVELS, D, hid)
    grad_down_left = jnp.dot(cotangent, down_code.T, preferred_element_type=jnp.float32)
    grad_down_right = jnp.dot(hidden_flat, down_back.T, preferred_element_type=jnp.float32)
    return (output, input_grad, grad_up_diag, grad_up_cross, grad_up_left, grad_up_right, grad_down_diag, grad_down_cross, grad_down_left, grad_down_right)
```

```python
import functools

import jax
import jax.numpy as jnp
from jax import lax
from jax.experimental import pallas as pl
from jax.experimental.pallas import tpu as pltpu
from jax.sharding import PartitionSpec as P


def swapped(block, axis, apart):
    count = lax.axis_size(axis)
    route = []
    for low in range(count):
        high = low | 1 << apart
        if high != low and high < count:
            route += [(low, high), (high, low)]
    return lax.ppermute(block, axis, route)


def after(block, *earlier):
    return lax.optimization_barrier((block,) + earlier)[0]


def outer(total, left, right, by_column):
    extent = (right if by_column else left)[0].shape[0]
    tile = 256 if extent % 256 == 0 else extent

    def step(index, carry):
        span = pl.ds(pl.multiple_of(index * tile, tile), tile)
        value = None
        for one, two in zip(left, right):
            term = against(one[...], two[span]) if by_column else against(one[span], two[...])
            value = term if value is None else value + term
        if by_column:
            total[:, span] = value
        else:
            total[span] = value
        return carry

    lax.fori_loop(0, extent // tile, step, 0)


def chunk_kernel(level_bits, columns, feats, earlier, *refs):
    blocks = len(columns)
    levels = len(level_bits)
    sources, refs = refs[:blocks], refs[blocks:]
    stored, refs = refs[: 6 + earlier], refs[6 + earlier :]
    landing, refs = refs[:blocks], refs[blocks:]
    hidden, pre_grad, out_near, in_near, payload, code = refs[:6]
    refs = refs[6:]
    if earlier:
        grads, refs = refs[0], refs[1:]
    loaded = refs[: 6 + earlier]
    far_send, far_recv, local = refs[6 + earlier :]
    up, up_turned, down, down_turned, ins, cots = loaded[:6]
    place = lax.axis_index("feat")
    width = ins.shape[1]
    code_rows = feats * (levels + 1)
    rank = ins.shape[0] - code_rows
    partners = []
    for bit in level_bits:
        mine = lax.rem(place // (1 << bit), 2)
        partners.append(place + (1 - 2 * mine) * (1 << bit))
    loads = []
    for index, (source, target) in enumerate(zip(stored, loaded)):
        copy = pltpu.make_async_copy(source, target, local.at[index])
        copy.start()
        loads.append(copy)
    barrier = pltpu.get_barrier_semaphore()
    for partner in partners:
        pl.semaphore_signal(
            barrier, inc=1, device_id={"feat": partner}, device_id_type=pl.DeviceIdType.MESH
        )
    pl.semaphore_wait(barrier, levels)
    started = []
    for index, (start, size) in enumerate(columns):
        for level in reversed(range(levels)):
            source = sources[index]
            if len(source.shape) == 3:
                source = source.at[level]
            spot = index * levels + level
            copy = pltpu.make_async_remote_copy(
                src_ref=source.at[:, start : start + size],
                dst_ref=landing[index].at[level],
                send_sem=far_send.at[spot],
                recv_sem=far_recv.at[spot],
                device_id={"feat": partners[level]},
                device_id_type=pl.DeviceIdType.MESH,
            )
            copy.start()
            started.append(copy)
    for copy in loads:
        copy.wait()
    tile = 256 if width % 256 == 0 else width

    def step(index, carry):
        span = pl.ds(pl.multiple_of(index * tile, tile), tile)
        later = pl.ds(pl.multiple_of(width + index * tile, tile), tile)
        active, slope = activate(dot(up[...], ins[:, span]))
        active = active.astype(jnp.bfloat16)
        hidden[:, span] = active
        outs = dot(down[...], active)
        grad = (dot(down_turned[...], cots[:, span]) * slope).astype(jnp.bfloat16)
        pre_grad[:, span] = grad
        in_grads = dot(up_turned[...], grad)
        out_near[:, span] = outs[:feats]
        in_near[:, span] = in_grads[:feats]
        for level in range(levels):
            rows = slice(feats * (level + 1), feats * (level + 2))
            payload[level, :, span] = outs[rows].astype(jnp.bfloat16)
            payload[level, :, later] = in_grads[rows].astype(jnp.bfloat16)
        code[:rank, span] = outs[code_rows:]
        code[rank:, span] = in_grads[code_rows:]
        return carry

    lax.fori_loop(0, width // tile, step, 0)
    if earlier:
        outer(grads, (loaded[6], cots), (loaded[7], hidden), True)
    for copy in started:
        copy.wait()


def chunk_step(level_bits, blocks, stored, feats, number):
    levels = len(level_bits)
    hid = stored[0].shape[0]
    rows, width = stored[4].shape
    rank = rows - feats * (levels + 1)
    earlier = len(stored) - 6
    copies = len(blocks) * levels
    made = [
        ((hid, width), jnp.bfloat16),
        ((hid, width), jnp.bfloat16),
        ((feats, width), jnp.float32),
        ((feats, width), jnp.float32),
        ((levels, feats, 2 * width), jnp.bfloat16),
        ((2 * rank, width), jnp.float32),
    ]
    if earlier:
        made.append(((rows, hid), jnp.float32))
    found = pl.pallas_call(
        functools.partial(
            chunk_kernel, tuple(level_bits), tuple(block[1:] for block in blocks), feats, earlier
        ),
        out_shape=[
            jax.ShapeDtypeStruct((levels, block.shape[-2], size), block.dtype)
            for block, _, size in blocks
        ]
        + [jax.ShapeDtypeStruct(*one) for one in made],
        in_specs=[pl.BlockSpec(memory_space=pl.ANY)] * (len(blocks) + len(stored)),
        out_specs=[pl.BlockSpec(memory_space=pl.ANY)] * len(blocks)
        + [pl.BlockSpec(memory_space=pltpu.VMEM)] * len(made),
        scratch_shapes=[pltpu.VMEM(block.shape, block.dtype) for block in stored]
        + [
            pltpu.SemaphoreType.DMA((copies,)),
            pltpu.SemaphoreType.DMA((copies,)),
            pltpu.SemaphoreType.DMA((len(stored),)),
        ],
        compiler_params=pltpu.CompilerParams(
            collective_id=number, has_side_effects=True, vmem_limit_bytes=60 * 2**20
        ),
    )(*[block[0] for block in blocks], *stored)
    return found[: len(blocks)], found[len(blocks) :]


def exchange_kernel(level_bits, sizes, early, pairs, part, *refs):
    blocks = len(sizes)
    levels = len(level_bits)
    sources, refs = refs[:blocks], refs[blocks:]
    stored, refs = refs[:pairs], refs[pairs:]
    code, landing, refs = refs[0], refs[1 : blocks + 1], refs[blocks + 1 :]
    if pairs:
        grads, refs = refs[0], refs[1:]
    work, received, gathered, send, recv, far_send, far_recv = refs[:7]
    loaded = refs[7 : 7 + pairs]
    count = part.shape[0]
    bits = count.bit_length() - 1
    place = lax.axis_index("feat")

    def partner(bit):
        mine = lax.rem(place // (1 << bit), 2)
        return mine, place + (1 - 2 * mine) * (1 << bit)

    def far(index, level):
        source = sources[index]
        if len(source.shape) == 3:
            source = source.at[level]
        spot = index * levels + level
        return pltpu.make_async_remote_copy(
            src_ref=source.at[:, : sizes[index]],
            dst_ref=landing[index].at[level],
            send_sem=far_send.at[spot],
            recv_sem=far_recv.at[spot],
            device_id={"feat": partner(level_bits[level])[1]},
            device_id_type=pl.DeviceIdType.MESH,
        )

    def near(source, target, step, bit):
        return pltpu.make_async_remote_copy(
            src_ref=source,
            dst_ref=target,
            send_sem=send.at[step],
            recv_sem=recv.at[step],
            device_id={"feat": partner(bit)[1]},
            device_id_type=pl.DeviceIdType.MESH,
        )

    barrier = pltpu.get_barrier_semaphore()
    for bit in range(bits):
        pl.semaphore_signal(
            barrier,
            inc=1,
            device_id={"feat": partner(bit)[1]},
            device_id_type=pl.DeviceIdType.MESH,
        )
    pl.semaphore_wait(barrier, bits)

    copies = []
    pending = [(index, level) for index in range(blocks) for level in reversed(range(levels))]
    started = []

    def launch(wanted):
        for item in list(pending):
            if wanted(*item):
                copy = far(*item)
                copy.start()
                started.append(copy)
                pending.remove(item)

    loads = [
        pltpu.make_async_copy(source, target, refs[-1].at[index])
        for index, (source, target) in enumerate(zip(stored, loaded))
    ]
    for copy in loads:
        copy.start()
    top = levels // 2
    launch(lambda index, level: index < early and level >= top)
    base = 0
    offset = 0
    length = count
    for bit in range(bits):
        mine = partner(bit)[0]
        half = length // 2
        keep = base + mine * half
        away = base + (1 - mine) * half
        held = part if bit == 0 else work
        copy = near(
            held.at[pl.ds(away, half)], received.at[pl.ds(offset, half)], bit, bit
        )
        copy.start()
        copies.append(copy)
        if bit == bits - levels + top:
            launch(lambda index, level: level < top)
        copy.wait_recv()
        work[pl.ds(keep, half)] = (
            held[pl.ds(keep, half)] + received[pl.ds(offset, half)]
        )
        base, offset, length = keep, offset + half, half
    launch(lambda index, level: index < early + 1)
    gathered[pl.ds(base, 1)] = work[pl.ds(base, 1)].astype(jnp.bfloat16)
    for bit in reversed(range(bits)):
        mine = partner(bit)[0]
        span = pl.ds(base, length)
        copy = near(gathered.at[span], gathered.at[span], 2 * bits - 1 - bit, bit)
        copy.start()
        copies.append(copy)
        copy.wait_recv()
        base, length = base - mine * length, 2 * length
        if bit == bits - levels + top:
            launch(lambda index, level: True)
    code[...] = gathered[...]
    for copy in loads:
        copy.wait()
    if pairs:
        outer(grads, loaded[: pairs // 2], loaded[pairs // 2 :], False)
    for copy in copies:
        copy.wait_send()
    for copy in started:
        copy.wait()


def exchange(part, level_bits, blocks, early, number, stored=()):
    count = lax.axis_size("feat")
    bits = count.bit_length() - 1
    levels = len(level_bits)
    flat = part.reshape(count, 16, -1)
    sizes = tuple(size for _, size in blocks)
    copies = max(1, len(blocks) * levels)
    found = pl.pallas_call(
        functools.partial(exchange_kernel, tuple(level_bits), sizes, early, len(stored)),
        out_shape=[jax.ShapeDtypeStruct(flat.shape, jnp.bfloat16)]
        + [
            jax.ShapeDtypeStruct((levels, block.shape[-2], size), block.dtype)
            for block, size in blocks
        ]
        + [
            jax.ShapeDtypeStruct((stored[0].shape[0], stored[-1].shape[0]), jnp.float32)
            for _ in stored[:1]
        ],
        in_specs=[pl.BlockSpec(memory_space=pltpu.VMEM)]
        + [pl.BlockSpec(memory_space=pl.ANY)] * (len(blocks) + len(stored)),
        out_specs=[pl.BlockSpec(memory_space=pltpu.VMEM)]
        + [pl.BlockSpec(memory_space=pl.ANY)] * len(blocks)
        + [pl.BlockSpec(memory_space=pltpu.VMEM) for _ in stored[:1]],
        scratch_shapes=[
            pltpu.VMEM(flat.shape, jnp.float32),
            pltpu.VMEM(flat.shape, jnp.float32),
            pltpu.VMEM(flat.shape, jnp.bfloat16),
            pltpu.SemaphoreType.DMA((2 * bits,)),
            pltpu.SemaphoreType.DMA((2 * bits,)),
            pltpu.SemaphoreType.DMA((copies,)),
            pltpu.SemaphoreType.DMA((copies,)),
        ]
        + [pltpu.VMEM(block.shape, block.dtype) for block in stored]
        + [pltpu.SemaphoreType.DMA((max(1, len(stored)),))],
        compiler_params=pltpu.CompilerParams(
            collective_id=number, has_side_effects=True, vmem_limit_bytes=56 * 2**20
        ),
    )(flat, *[block for block, _ in blocks], *stored)
    return found[0].reshape(part.shape), found[1:]


def activate(values):
    scale = (2.0 / jnp.pi) ** 0.5
    squares = values * values
    curve = jnp.tanh(scale * values * (1.0 + 0.044715 * squares))
    half = 0.5 * (1.0 + curve)
    slope = half + 0.5 * values * (1.0 - curve * curve) * (
        scale * (1.0 + 3 * 0.044715 * squares)
    )
    return values * half, slope


def dot(left, right):
    return jnp.dot(left, right, preferred_element_type=jnp.float32)


def across(left, right):
    return lax.dot_general(
        left, right, (((0,), (0,)), ((), ())), preferred_element_type=jnp.float32
    )


def against(left, right):
    return lax.dot_general(
        left, right, (((1,), (1,)), ((), ())), preferred_element_type=jnp.float32
    )


def on_device(
    inputs,
    pattern,
    rank_mask,
    up_diag,
    up_cross,
    up_left,
    up_right,
    down_diag,
    down_cross,
    down_left,
    down_right,
    cotangent,
):
    levels = up_cross.shape[0]
    rank = rank_mask.shape[0]
    feats, tokens = inputs.shape
    hid = up_diag.shape[0]
    chunks = 2
    width = tokens // chunks
    highest = lax.axis_size("feat").bit_length() - 1
    level_bits = [highest - levels + level for level in range(levels)]
    order = list(range(levels))[::-1]
    gate_values = pattern.astype(jnp.float32)
    gate_blocks = pattern.astype(jnp.bfloat16)[:, :, None]
    keep = rank_mask.astype(jnp.bfloat16)[:, None]
    spans = [(feats * level, feats * (level + 1)) for level in range(levels + 1)]
    code_rows = feats * (levels + 1)

    def swap(block, level):
        return swapped(block, "feat", level_bits[level])

    def piece(block, chunk):
        return block[:, chunk * width : (chunk + 1) * width]

    down_gated = down_cross * gate_blocks
    codes, (in_first, down_far, cot_first) = exchange(
        jnp.concatenate([across(up_right, inputs), across(down_left, cotangent)]),
        level_bits,
        [(inputs, width), (down_gated, hid), (cotangent, width)],
        1,
        0,
    )
    up_code = codes[:rank] * keep
    down_back = codes[rank:] * keep
    up_gated = up_cross * gate_blocks
    up_all = jnp.concatenate(
        [up_diag] + [up_gated[level] for level in range(levels)] + [up_left], axis=1
    )
    down_all = jnp.concatenate(
        [down_diag] + [down_far[level] for level in range(levels)] + [jnp.transpose(down_right)]
    )

    up_turned = jnp.transpose(up_all)
    down_turned = jnp.transpose(down_all)

    def gathered(near, far, code, chunk):
        return jnp.concatenate(
            [piece(near, chunk), far.reshape(levels * feats, width), piece(code, chunk)]
        )

    weights = [up_all, up_turned, down_all, down_turned]
    ins = [gathered(inputs, in_first, up_code, 0)]
    cots = [gathered(cotangent, cot_first, down_back, 0)]
    (in_second, cot_second), one = chunk_step(
        level_bits,
        [(inputs, width, width), (cotangent, width, width)],
        weights + [ins[0], cots[0]],
        feats,
        2,
    )
    ins.append(gathered(inputs, in_second, up_code, 1))
    cots.append(gathered(cotangent, cot_second, down_back, 1))
    (back_first,), two = chunk_step(
        level_bits,
        [(one[4], 0, 2 * width)],
        weights + [ins[1], cots[1], cots[0], one[0]],
        feats,
        3,
    )
    grads_down = two[6]
    grads_sent = grads_down[feats:code_rows].astype(jnp.bfloat16).reshape(levels, feats, hid)
    codes, (back_second, grad_parts, grads_up) = exchange(
        jnp.concatenate([one[5], two[5]], axis=1),
        level_bits,
        [(two[4], 2 * width), (grads_sent, hid)],
        1,
        1,
        (one[1], two[1], ins[0], ins[1]),
    )
    out_near, in_near = [one[2], two[2]], [one[3], two[3]]
    back = [back_first, back_second]
    down_code = codes[:rank] * keep
    up_back = codes[rank:] * keep

    grad_up_diag = grads_up[:, :feats]
    grad_up_cross = jnp.stack(
        [
            gate_values[level, 0] * grads_up[:, slice(*spans[level + 1])]
            for level in range(levels)
        ]
    )
    grad_up_left = grads_up[:, code_rows:]
    grad_down_diag = grads_down[:feats]
    grad_down_right = jnp.transpose(grads_down[code_rows:])
    grad_down_cross = jnp.stack(
        [gate_values[level, 0] * grad_parts[level].astype(jnp.float32) for level in range(levels)]
    )
    grad_down_left = against(cotangent, down_code)
    grad_up_right = against(inputs, up_back)

    output, input_grad = [], []
    for chunk in range(chunks):
        result = out_near[chunk] + dot(down_left, piece(down_code, chunk))
        in_grad = in_near[chunk] + dot(up_right, piece(up_back, chunk))
        for level in order[::-1]:
            result = result + back[chunk][level][:, :width].astype(jnp.float32)
            in_grad = in_grad + back[chunk][level][:, width:].astype(jnp.float32)
        output.append(result.astype(jnp.bfloat16))
        input_grad.append(in_grad.astype(jnp.bfloat16))
    output = jnp.concatenate(output, axis=1)
    input_grad = jnp.concatenate(input_grad, axis=1)
    return (
        output,
        input_grad,
        grad_up_diag,
        grad_up_cross,
        grad_up_left,
        grad_up_right,
        grad_down_diag,
        grad_down_cross,
        grad_down_left,
        grad_down_right,
    )


def solution(mesh):
    in_specs = (
        P("feat", "grp"),
        P(None, "feat"),
        P(),
        P("feat", None),
        P(None, "feat", None),
        P("feat", None),
        P("feat", None),
        P("feat", None),
        P(None, "feat", None),
        P("feat", None),
        P("feat", None),
        P("feat", "grp"),
    )
    out_specs = (
        P("feat", "grp"),
        P("feat", "grp"),
        P("feat", "grp"),
        P(None, "feat", "grp"),
        P("feat", "grp"),
        P("feat", "grp"),
        P("feat", "grp"),
        P(None, "feat", "grp"),
        P("feat", "grp"),
        P("feat", "grp"),
    )
    return jax.shard_map(
        on_device, mesh=mesh, in_specs=in_specs, out_specs=out_specs, check_vma=False
    )
```

```python
import functools

import jax
import jax.numpy as jnp
from jax import lax
from jax.experimental import pallas as pl
from jax.experimental.pallas import tpu as pltpu
from jax.sharding import PartitionSpec as P


def swapped(block, axis, apart):
    count = lax.axis_size(axis)
    route = []
    for low in range(count):
        high = low | 1 << apart
        if high != low and high < count:
            route += [(low, high), (high, low)]
    return lax.ppermute(block, axis, route)


def after(block, *earlier):
    return lax.optimization_barrier((block,) + earlier)[0]


def outer(total, left, right, by_column):
    extent = (right if by_column else left)[0].shape[0]
    tile = 256 if extent % 256 == 0 else extent

    def step(index, carry):
        span = pl.ds(pl.multiple_of(index * tile, tile), tile)
        value = None
        for one, two in zip(left, right):
            term = against(one[...], two[span]) if by_column else against(one[span], two[...])
            value = term if value is None else value + term
        if by_column:
            total[:, span] = value
        else:
            diag, cross, low, gate = total
            feats = diag.shape[1]
            levels = cross.shape[0]
            diag[span] = value[:, :feats]
            for level in range(levels):
                cross[level, span] = (
                    gate[level, 0] * value[:, feats * (level + 1) : feats * (level + 2)]
                )
            low[span] = value[:, feats * (levels + 1) :]
        return carry

    lax.fori_loop(0, extent // tile, step, 0)


def chunk_kernel(level_bits, columns, feats, earlier, *refs):
    blocks = len(columns)
    levels = len(level_bits)
    sources, refs = refs[:blocks], refs[blocks:]
    stored, refs = refs[: 6 + earlier], refs[6 + earlier :]
    landing, refs = refs[:blocks], refs[blocks:]
    hidden, pre_grad, out_near, in_near, payload, code = refs[:6]
    refs = refs[6:]
    if earlier:
        grads, refs = refs[0], refs[1:]
    loaded = refs[: 6 + earlier]
    far_send, far_recv, local = refs[6 + earlier :]
    up, up_turned, down, down_turned, ins, cots = loaded[:6]
    place = lax.axis_index("feat")
    width = ins.shape[1]
    code_rows = feats * (levels + 1)
    rank = ins.shape[0] - code_rows
    partners = []
    for bit in level_bits:
        mine = lax.rem(place // (1 << bit), 2)
        partners.append(place + (1 - 2 * mine) * (1 << bit))
    loads = []
    for index, (source, target) in enumerate(zip(stored, loaded)):
        copy = pltpu.make_async_copy(source, target, local.at[index])
        copy.start()
        loads.append(copy)
    barrier = pltpu.get_barrier_semaphore()
    for partner in partners:
        pl.semaphore_signal(
            barrier, inc=1, device_id={"feat": partner}, device_id_type=pl.DeviceIdType.MESH
        )
    pl.semaphore_wait(barrier, levels)
    started = []
    for index, (start, size) in enumerate(columns):
        for level in reversed(range(levels)):
            source = sources[index]
            if len(source.shape) == 3:
                source = source.at[level]
            spot = index * levels + level
            copy = pltpu.make_async_remote_copy(
                src_ref=source.at[:, start : start + size],
                dst_ref=landing[index].at[level],
                send_sem=far_send.at[spot],
                recv_sem=far_recv.at[spot],
                device_id={"feat": partners[level]},
                device_id_type=pl.DeviceIdType.MESH,
            )
            copy.start()
            started.append(copy)
    for copy in loads:
        copy.wait()
    tile = 256 if width % 256 == 0 else width

    def step(index, carry):
        span = pl.ds(pl.multiple_of(index * tile, tile), tile)
        later = pl.ds(pl.multiple_of(width + index * tile, tile), tile)
        active, slope = activate(dot(up[...], ins[:, span]))
        active = active.astype(jnp.bfloat16)
        hidden[:, span] = active
        outs = dot(down[...], active)
        grad = (dot(down_turned[...], cots[:, span]) * slope).astype(jnp.bfloat16)
        pre_grad[:, span] = grad
        in_grads = dot(up_turned[...], grad)
        out_near[:, span] = outs[:feats]
        in_near[:, span] = in_grads[:feats]
        for level in range(levels):
            rows = slice(feats * (level + 1), feats * (level + 2))
            payload[level, :, span] = outs[rows].astype(jnp.bfloat16)
            payload[level, :, later] = in_grads[rows].astype(jnp.bfloat16)
        code[:rank, span] = outs[code_rows:]
        code[rank:, span] = in_grads[code_rows:]
        return carry

    lax.fori_loop(0, width // tile, step, 0)
    if earlier:
        outer(grads, (loaded[6], cots), (loaded[7], hidden), True)
    for copy in started:
        copy.wait()


def chunk_step(level_bits, blocks, stored, feats, number):
    levels = len(level_bits)
    hid = stored[0].shape[0]
    rows, width = stored[4].shape
    rank = rows - feats * (levels + 1)
    earlier = len(stored) - 6
    copies = len(blocks) * levels
    made = [
        ((hid, width), jnp.bfloat16),
        ((hid, width), jnp.bfloat16),
        ((feats, width), jnp.float32),
        ((feats, width), jnp.float32),
        ((levels, feats, 2 * width), jnp.bfloat16),
        ((2 * rank, width), jnp.float32),
    ]
    if earlier:
        made.append(((rows, hid), jnp.float32))
    found = pl.pallas_call(
        functools.partial(
            chunk_kernel, tuple(level_bits), tuple(block[1:] for block in blocks), feats, earlier
        ),
        out_shape=[
            jax.ShapeDtypeStruct((levels, block.shape[-2], size), block.dtype)
            for block, _, size in blocks
        ]
        + [jax.ShapeDtypeStruct(*one) for one in made],
        in_specs=[pl.BlockSpec(memory_space=pl.ANY)] * (len(blocks) + len(stored)),
        out_specs=[pl.BlockSpec(memory_space=pl.ANY)] * len(blocks)
        + [pl.BlockSpec(memory_space=pltpu.VMEM)] * len(made),
        scratch_shapes=[pltpu.VMEM(block.shape, block.dtype) for block in stored]
        + [
            pltpu.SemaphoreType.DMA((copies,)),
            pltpu.SemaphoreType.DMA((copies,)),
            pltpu.SemaphoreType.DMA((len(stored),)),
        ],
        compiler_params=pltpu.CompilerParams(
            collective_id=number, has_side_effects=True, vmem_limit_bytes=60 * 2**20
        ),
    )(*[block[0] for block in blocks], *stored)
    return found[: len(blocks)], found[len(blocks) :]


def exchange_kernel(level_bits, sizes, early, pairs, part, gate, *refs):
    blocks = len(sizes)
    levels = len(level_bits)
    sources, refs = refs[:blocks], refs[blocks:]
    stored, refs = refs[:pairs], refs[pairs:]
    code, landing, refs = refs[0], refs[1 : blocks + 1], refs[blocks + 1 :]
    if pairs:
        grads, refs = refs[:3] + (gate,), refs[3:]
    work, received, gathered, send, recv, far_send, far_recv = refs[:7]
    loaded = refs[7 : 7 + pairs]
    count = part.shape[0]
    bits = count.bit_length() - 1
    place = lax.axis_index("feat")

    def partner(bit):
        mine = lax.rem(place // (1 << bit), 2)
        return mine, place + (1 - 2 * mine) * (1 << bit)

    def far(index, level):
        source = sources[index]
        if len(source.shape) == 3:
            source = source.at[level]
        spot = index * levels + level
        return pltpu.make_async_remote_copy(
            src_ref=source.at[:, : sizes[index]],
            dst_ref=landing[index].at[level],
            send_sem=far_send.at[spot],
            recv_sem=far_recv.at[spot],
            device_id={"feat": partner(level_bits[level])[1]},
            device_id_type=pl.DeviceIdType.MESH,
        )

    def near(source, target, step, bit):
        return pltpu.make_async_remote_copy(
            src_ref=source,
            dst_ref=target,
            send_sem=send.at[step],
            recv_sem=recv.at[step],
            device_id={"feat": partner(bit)[1]},
            device_id_type=pl.DeviceIdType.MESH,
        )

    barrier = pltpu.get_barrier_semaphore()
    for bit in range(bits):
        pl.semaphore_signal(
            barrier,
            inc=1,
            device_id={"feat": partner(bit)[1]},
            device_id_type=pl.DeviceIdType.MESH,
        )
    pl.semaphore_wait(barrier, bits)

    copies = []
    pending = [(index, level) for index in range(blocks) for level in reversed(range(levels))]
    started = []

    def launch(wanted):
        for item in list(pending):
            if wanted(*item):
                copy = far(*item)
                copy.start()
                started.append(copy)
                pending.remove(item)

    loads = [
        pltpu.make_async_copy(source, target, refs[-1].at[index])
        for index, (source, target) in enumerate(zip(stored, loaded))
    ]
    for copy in loads:
        copy.start()
    top = levels // 2
    launch(lambda index, level: index < early and level >= top)
    base = 0
    offset = 0
    length = count
    for bit in range(bits):
        mine = partner(bit)[0]
        half = length // 2
        keep = base + mine * half
        away = base + (1 - mine) * half
        held = part if bit == 0 else work
        copy = near(
            held.at[pl.ds(away, half)], received.at[pl.ds(offset, half)], bit, bit
        )
        copy.start()
        copies.append(copy)
        if bit == bits - levels + top:
            launch(lambda index, level: level < top)
            for load in loads:
                load.wait()
            if pairs:
                outer(grads, loaded[: pairs // 2], loaded[pairs // 2 :], False)
        copy.wait_recv()
        work[pl.ds(keep, half)] = (
            held[pl.ds(keep, half)] + received[pl.ds(offset, half)]
        )
        base, offset, length = keep, offset + half, half
    launch(lambda index, level: index < early + 1)
    gathered[pl.ds(base, 1)] = work[pl.ds(base, 1)].astype(jnp.bfloat16)
    for bit in reversed(range(bits)):
        mine = partner(bit)[0]
        span = pl.ds(base, length)
        copy = near(gathered.at[span], gathered.at[span], 2 * bits - 1 - bit, bit)
        copy.start()
        copies.append(copy)
        copy.wait_recv()
        base, length = base - mine * length, 2 * length
        if bit == bits - levels + top:
            launch(lambda index, level: True)
    code[...] = gathered[...]
    for copy in copies:
        copy.wait_send()
    for copy in started:
        copy.wait()


def exchange(part, gate, level_bits, blocks, early, number, stored=()):
    count = lax.axis_size("feat")
    bits = count.bit_length() - 1
    levels = len(level_bits)
    flat = part.reshape(count, 16, -1)
    sizes = tuple(size for _, size in blocks)
    copies = max(1, len(blocks) * levels)
    made = []
    if stored:
        hid, feats = stored[0].shape[0], blocks[0][0].shape[-2]
        rank = stored[-1].shape[0] - feats * (levels + 1)
        made = [(hid, feats), (levels, hid, feats), (hid, rank)]
    found = pl.pallas_call(
        functools.partial(exchange_kernel, tuple(level_bits), sizes, early, len(stored)),
        out_shape=[jax.ShapeDtypeStruct(flat.shape, jnp.bfloat16)]
        + [
            jax.ShapeDtypeStruct((levels, block.shape[-2], size), block.dtype)
            for block, size in blocks
        ]
        + [
            jax.ShapeDtypeStruct(shape, jnp.float32) for shape in made
        ],
        in_specs=[
            pl.BlockSpec(memory_space=pltpu.VMEM),
            pl.BlockSpec(memory_space=pltpu.SMEM),
        ]
        + [pl.BlockSpec(memory_space=pl.ANY)] * (len(blocks) + len(stored)),
        out_specs=[pl.BlockSpec(memory_space=pltpu.VMEM)]
        + [pl.BlockSpec(memory_space=pl.ANY)] * len(blocks)
        + [pl.BlockSpec(memory_space=pltpu.VMEM) for _ in made],
        scratch_shapes=[
            pltpu.VMEM(flat.shape, jnp.float32),
            pltpu.VMEM(flat.shape, jnp.float32),
            pltpu.VMEM(flat.shape, jnp.bfloat16),
            pltpu.SemaphoreType.DMA((2 * bits,)),
            pltpu.SemaphoreType.DMA((2 * bits,)),
            pltpu.SemaphoreType.DMA((copies,)),
            pltpu.SemaphoreType.DMA((copies,)),
        ]
        + [pltpu.VMEM(block.shape, block.dtype) for block in stored]
        + [pltpu.SemaphoreType.DMA((max(1, len(stored)),))],
        compiler_params=pltpu.CompilerParams(
            collective_id=number, has_side_effects=True, vmem_limit_bytes=56 * 2**20
        ),
    )(flat, gate, *[block for block, _ in blocks], *stored)
    return found[0].reshape(part.shape), found[1:]


def activate(values):
    scale = (2.0 / jnp.pi) ** 0.5
    squares = values * values
    curve = jnp.tanh(scale * values * (1.0 + 0.044715 * squares))
    half = 0.5 * (1.0 + curve)
    slope = half + 0.5 * values * (1.0 - curve * curve) * (
        scale * (1.0 + 3 * 0.044715 * squares)
    )
    return values * half, slope


def dot(left, right):
    return jnp.dot(left, right, preferred_element_type=jnp.float32)


def across(left, right):
    return lax.dot_general(
        left, right, (((0,), (0,)), ((), ())), preferred_element_type=jnp.float32
    )


def against(left, right):
    return lax.dot_general(
        left, right, (((1,), (1,)), ((), ())), preferred_element_type=jnp.float32
    )


def on_device(
    inputs,
    pattern,
    rank_mask,
    up_diag,
    up_cross,
    up_left,
    up_right,
    down_diag,
    down_cross,
    down_left,
    down_right,
    cotangent,
):
    levels = up_cross.shape[0]
    rank = rank_mask.shape[0]
    feats, tokens = inputs.shape
    hid = up_diag.shape[0]
    chunks = 2
    width = tokens // chunks
    highest = lax.axis_size("feat").bit_length() - 1
    level_bits = [highest - levels + level for level in range(levels)]
    order = list(range(levels))[::-1]
    gate_values = pattern.astype(jnp.float32)
    gate_blocks = pattern.astype(jnp.bfloat16)[:, :, None]
    keep = rank_mask.astype(jnp.bfloat16)[:, None]
    spans = [(feats * level, feats * (level + 1)) for level in range(levels + 1)]
    code_rows = feats * (levels + 1)

    def swap(block, level):
        return swapped(block, "feat", level_bits[level])

    def piece(block, chunk):
        return block[:, chunk * width : (chunk + 1) * width]

    down_gated = down_cross * gate_blocks
    codes, (in_first, down_far, cot_first) = exchange(
        jnp.concatenate([across(up_right, inputs), across(down_left, cotangent)]),
        gate_values,
        level_bits,
        [(inputs, width), (down_gated, hid), (cotangent, width)],
        1,
        0,
    )
    up_code = codes[:rank] * keep
    down_back = codes[rank:] * keep
    up_gated = up_cross * gate_blocks
    up_all = jnp.concatenate(
        [up_diag] + [up_gated[level] for level in range(levels)] + [up_left], axis=1
    )
    down_all = jnp.concatenate(
        [down_diag] + [down_far[level] for level in range(levels)] + [jnp.transpose(down_right)]
    )

    up_turned = jnp.transpose(up_all)
    down_turned = jnp.transpose(down_all)

    def gathered(near, far, code, chunk):
        return jnp.concatenate(
            [piece(near, chunk), far.reshape(levels * feats, width), piece(code, chunk)]
        )

    weights = [up_all, up_turned, down_all, down_turned]
    ins = [gathered(inputs, in_first, up_code, 0)]
    cots = [gathered(cotangent, cot_first, down_back, 0)]
    (in_second, cot_second), one = chunk_step(
        level_bits,
        [(inputs, width, width), (cotangent, width, width)],
        weights + [ins[0], cots[0]],
        feats,
        2,
    )
    ins.append(gathered(inputs, in_second, up_code, 1))
    cots.append(gathered(cotangent, cot_second, down_back, 1))
    (back_first,), two = chunk_step(
        level_bits,
        [(one[4], 0, 2 * width)],
        weights + [ins[1], cots[1], cots[0], one[0]],
        feats,
        3,
    )
    grads_down = two[6]
    grads_sent = grads_down[feats:code_rows].astype(jnp.bfloat16).reshape(levels, feats, hid)
    codes, (back_second, grad_parts, grad_up_diag, grad_up_cross, grad_up_left) = exchange(
        jnp.concatenate([one[5], two[5]], axis=1),
        gate_values,
        level_bits,
        [(two[4], 2 * width), (grads_sent, hid)],
        2,
        1,
        (one[1], two[1], ins[0], ins[1]),
    )
    out_near, in_near = [one[2], two[2]], [one[3], two[3]]
    back = [back_first, back_second]
    down_code = codes[:rank] * keep
    up_back = codes[rank:] * keep

    grad_down_diag = grads_down[:feats]
    grad_down_right = jnp.transpose(grads_down[code_rows:])
    grad_down_cross = jnp.stack(
        [gate_values[level, 0] * grad_parts[level].astype(jnp.float32) for level in range(levels)]
    )
    grad_down_left = against(cotangent, down_code)
    grad_up_right = against(inputs, up_back)

    output, input_grad = [], []
    for chunk in range(chunks):
        result = out_near[chunk] + dot(down_left, piece(down_code, chunk))
        in_grad = in_near[chunk] + dot(up_right, piece(up_back, chunk))
        for level in order[::-1]:
            result = result + back[chunk][level][:, :width].astype(jnp.float32)
            in_grad = in_grad + back[chunk][level][:, width:].astype(jnp.float32)
        output.append(result.astype(jnp.bfloat16))
        input_grad.append(in_grad.astype(jnp.bfloat16))
    output = jnp.concatenate(output, axis=1)
    input_grad = jnp.concatenate(input_grad, axis=1)
    return (
        output,
        input_grad,
        grad_up_diag,
        grad_up_cross,
        grad_up_left,
        grad_up_right,
        grad_down_diag,
        grad_down_cross,
        grad_down_left,
        grad_down_right,
    )


def solution(mesh):
    in_specs = (
        P("feat", "grp"),
        P(None, "feat"),
        P(),
        P("feat", None),
        P(None, "feat", None),
        P("feat", None),
        P("feat", None),
        P("feat", None),
        P(None, "feat", None),
        P("feat", None),
        P("feat", None),
        P("feat", "grp"),
    )
    out_specs = (
        P("feat", "grp"),
        P("feat", "grp"),
        P("feat", "grp"),
        P(None, "feat", "grp"),
        P("feat", "grp"),
        P("feat", "grp"),
        P("feat", "grp"),
        P(None, "feat", "grp"),
        P("feat", "grp"),
        P("feat", "grp"),
    )
    return jax.shard_map(
        on_device, mesh=mesh, in_specs=in_specs, out_specs=out_specs, check_vma=False
    )
```
